32 devices in a mesh: dp: 4 (over z), seq: 8 (over y, x, core).
Axes of the slice: x: 2, y: 2, z: 4, core: 2. Of those that a mesh axis runs over, the one named last changes fastest.
Arguments:
- embeddings: bfloat16 [4, 1024, 1536], P('dp', 'seq'), may hold values from -6 to 6
- conv_one: bfloat16 [3, 1536, 1536], P(None, 'dp'), may hold values from -0.09375 to 0.09375
- conv_two: bfloat16 [3, 1536, 1536], P(None, 'dp'), may hold values from -0.09375 to 0.09375
- head_weight: bfloat16 [1536, 3072], P(None, 'dp'), may hold values from -4 to 4
- counts: int32 [4, 1024, 3072], P(None, 'seq', 'dp'), may hold values from 0 to 12
- dilation: int32 [2], replicated, may hold values from 1 to 32, as said below
Outputs:
- track_loss: float32 [4, 3072], P(None, 'dp')
- grad_head: float32 [1536, 3072], P('seq', 'dp')
- grad_one: float32 [3, 1536, 1536], P(None, 'seq', 'dp')
- grad_two: float32 [3, 1536, 1536], P(None, 'seq', 'dp')
The draws below stay inside these ranges and needn't reach their ends.
Inputs may be any that keep to these rules, and one draw needn't show every extreme that they name: One of the two convolutions has dilation 32, the other a smaller one.
All inputs are finite; a program needn't handle non-finite values.
Results may differ from the reference program's by a relative error of at most 0.019.
The reference program's roundings to bfloat16 on the way count: a program that leaves them out, or rounds other values in their place, can miss the bound.
Values may be sent and summed in bfloat16 or wider, within the bound.
No kernel may reach another device: no remote copies, remote signals or barrier semaphores. Data moves between devices by JAX's collectives and lax.ppermute only.
A program may use at most 128 MiB of HBM per device.

```python
import math
import jax
import jax.numpy as jnp
from jax import lax

C = 1536
TR = 3072
DMAX = 32
BATCH = 4
BINS = 1024
N_DP = 4


def draw_head_weight(key, part):
    normal_part = jax.random.normal(key, (C, TR), jnp.float32) / math.sqrt(C)
    return normal_part.astype(jnp.bfloat16)


def draw_counts(key, part):
    position = jnp.arange(BINS, dtype=jnp.int32)
    ceiling = 4 + 9 * position // BINS
    return jax.random.randint(key, (BATCH, BINS, TR), 0, ceiling[None, :, None] + 1, dtype=jnp.int32)


def draw_dilation(key, part):
    second = jax.random.randint(jax.random.fold_in(key, 1), (), 1, DMAX, dtype=jnp.int32)
    chosen_slot = jax.random.randint(jax.random.fold_in(key, 2), (), 0, 2, dtype=jnp.int32)
    return jnp.where(jnp.arange(2, dtype=jnp.int32) == chosen_slot, DMAX, second).astype(jnp.int32)


def levels(key, extent, split, least, largest):
    def one(dim, parts):
        steps = jax.random.uniform(jax.random.fold_in(jax.random.fold_in(key, 6), dim), (parts,), jnp.float32, least / len(split), largest / len(split))
        return jnp.repeat(jnp.exp(steps), extent[dim] // parts).reshape((-1,) + (1,) * (len(extent) - dim - 1))

    gain = one(*split[0])
    for cut in split[1:]:
        gain = gain * one(*cut)
    return gain


def noise(rng, shape, spread, bound, pieces=(), kind=jnp.bfloat16):
    array = spread * jax.random.normal(rng, shape, jnp.float32)
    if pieces:
        array = array * levels(rng, shape, pieces, -0.22, 0.18)
    return jnp.clip(array, -bound, bound).astype(kind)


def setup_inputs(seed: int = 0) -> dict:
    seeds = jax.random.split(jax.random.key(seed), 7)
    return {
        "embeddings": noise(seeds[0], (BATCH, BINS, C), 1.0, 6.0, ((0, 4), (1, 8))),
        "conv_one": noise(seeds[1], (3, C, C), (3 * C) ** -0.5, 0.09375, ((1, 4),)),
        "conv_two": noise(seeds[2], (3, C, C), (3 * C) ** -0.5, 0.09375, ((1, 4),)),
        "head_weight": draw_head_weight(jax.random.fold_in(seeds[6], 71), 0),
        "counts": draw_counts(jax.random.fold_in(seeds[6], 71), 0),
        "dilation": draw_dilation(jax.random.fold_in(seeds[6], 71), 0),
    }


def activate(value):
    return jax.nn.gelu(value)

def padded_rows(field):
    return jnp.pad(field, ((DMAX, DMAX), (0, 0)))

def shifted_rows(padded, spacing, sign, tap_index):
    return lax.dynamic_slice_in_dim(padded, (DMAX + sign * (tap_index - 1) * spacing).astype(jnp.int32), BINS, 0)

def conv_forward(padded, weight, spacing):
    running = jnp.zeros((BINS, weight.shape[1]), jnp.float32)
    for tap_index in range(3):
        running = running + jnp.dot(shifted_rows(padded, spacing, 1, tap_index), weight[tap_index].T, preferred_element_type=jnp.float32)
    return running

def conv_weight_grad(padded, upstream, spacing):
    grads = []
    for tap_index in range(3):
        grads.append(jnp.dot(shifted_rows(padded, spacing, 1, tap_index).T, upstream, preferred_element_type=jnp.float32))
    return jnp.stack(grads)

def conv_input_grad(upstream, weight, spacing):
    padded = padded_rows(upstream)
    width = C // N_DP
    running = jnp.zeros((BINS, C), jnp.float32)
    for group_index in range(N_DP):
        partial_sum = jnp.zeros((BINS, C), jnp.float32)
        for tap_index in range(3):
            shifted = shifted_rows(padded, spacing, -1, tap_index)[:, group_index * width:(group_index + 1) * width]
            block_weight = weight[tap_index][group_index * width:(group_index + 1) * width, :]
            partial_sum = partial_sum + jnp.dot(shifted, block_weight, preferred_element_type=jnp.float32)
        rounded = lax.optimization_barrier(partial_sum.astype(jnp.bfloat16))
        running = running + rounded.astype(jnp.float32)
    return running

def head_input_grad(logit_grad, head_weight):
    width = TR // N_DP
    running = jnp.zeros((BINS, C), jnp.float32)
    for group_index in range(N_DP):
        partial_sum = jnp.dot(logit_grad[:, group_index * width:(group_index + 1) * width], head_weight[:, group_index * width:(group_index + 1) * width].T, preferred_element_type=jnp.float32)
        rounded = lax.optimization_barrier(partial_sum.astype(jnp.bfloat16))
        running = running + rounded.astype(jnp.float32)
    return running

def reference(embeddings, conv_one, conv_two, head_weight, counts, dilation):
    first_gap = dilation[0]
    second_gap = dilation[1]

    def one_sequence(inputs_one):
        field, count_rows = inputs_one
        targets = count_rows.astype(jnp.float32)
        framed_in = padded_rows(field)
        pre_one = conv_forward(framed_in, conv_one, first_gap)
        hidden_one = (field.astype(jnp.float32) + activate(pre_one)).astype(jnp.bfloat16)
        framed_one = padded_rows(hidden_one)
        pre_two = conv_forward(framed_one, conv_two, second_gap)
        hidden_two = (hidden_one.astype(jnp.float32) + activate(pre_two)).astype(jnp.bfloat16)
        logits = jnp.dot(hidden_two, head_weight, preferred_element_type=jnp.float32)
        peak_all = lax.optimization_barrier(jnp.max(logits, axis=0))
        exp_total = lax.optimization_barrier(jnp.sum(jnp.exp(logits - peak_all[None, :]), axis=0))
        log_total = peak_all + jnp.log(exp_total)
        count_total = lax.optimization_barrier(jnp.sum(targets, axis=0))
        cross_total = lax.optimization_barrier(jnp.sum(targets * logits, axis=0))
        track_loss = (count_total * log_total - cross_total) / BINS
        logit_grad = ((count_total[None, :] * jnp.exp(logits - log_total[None, :]) - targets) / BINS).astype(jnp.bfloat16)
        grad_head = jnp.dot(hidden_two.T, logit_grad, preferred_element_type=jnp.float32)
        grad_two_out = head_input_grad(logit_grad, head_weight)
        upstream_two = jax.vjp(activate, pre_two)[1](grad_two_out)[0].astype(jnp.bfloat16)
        grad_two = conv_weight_grad(framed_one, upstream_two, second_gap)
        grad_one_out = grad_two_out + conv_input_grad(upstream_two, conv_two, second_gap)
        upstream_one = jax.vjp(activate, pre_one)[1](grad_one_out)[0].astype(jnp.bfloat16)
        grad_one = conv_weight_grad(framed_in, upstream_one, first_gap)
        return (track_loss, grad_head, grad_one, grad_two)
    losses, heads, ones, twos = lax.map(one_sequence, (embeddings, counts))
    return (losses, lax.optimization_barrier(jnp.sum(heads, axis=0)), lax.optimization_barrier(jnp.sum(ones, axis=0)), lax.optimization_barrier(jnp.sum(twos, axis=0)))
```

```python
import jax
import jax.numpy as jnp
from jax import lax
from jax.sharding import PartitionSpec as P

DMAX = 32
GROUPS = 1
F32 = jnp.float32
BF16 = jnp.bfloat16


def dot(spec, a, b):
    return jnp.einsum(spec, a, b, preferred_element_type=F32)


def activate(value):
    return jax.nn.gelu(value)


def activate_grad(pre, upstream):
    return jax.vjp(activate, pre)[1](upstream)[0]


def send(value, axis, pairs):
    return lax.ppermute(value, axis, pairs)


def swap(value, axis, mask):
    return send(value, axis, [(i, i ^ mask) for i in range(lax.axis_size(axis))])


def line_gather(block):
    size = lax.axis_size("dp")
    if size != 4:
        return [block] + [swap(block, "dp", m) for m in range(1, size)]
    far = swap(block, "dp", 2)
    near = swap(block, "dp", 1)
    inner = send(block, "dp", [(1, 2), (2, 1)])
    outer = send(far, "dp", [(2, 3), (1, 0)])
    place = lax.axis_index("dp")
    middle = (place == 1) | (place == 2)
    return [block, near, far, jnp.where(middle, inner, outer)]


def line_scatter(chunks):
    size = lax.axis_size("dp")
    total = chunks[0].astype(F32)
    if size != 4:
        for m in range(1, size):
            total = total + swap(chunks[m], "dp", m).astype(F32)
        return total
    passed = send(chunks[3], "dp", [(0, 1), (3, 2)])
    near = swap(chunks[1], "dp", 1)
    far_chunk = (chunks[2].astype(F32) + passed.astype(F32)).astype(BF16)
    far = swap(far_chunk, "dp", 2)
    inner = send(chunks[3], "dp", [(1, 2), (2, 1)])
    return total + near.astype(F32) + inner.astype(F32) + far.astype(F32)


def with_halo(value):
    size, length = lax.axis_size("seq"), value.shape[1]
    up = [(i, i + 1) for i in range(size - 1)]
    down = [(j, i) for i, j in up]
    before = send(value[:, length - DMAX :], "seq", up)
    after = send(value[:, :DMAX], "seq", down)
    return jnp.concatenate([before, value, after], axis=1)


def shifted_taps(padded, spacing, sign):
    length = padded.shape[1] - 2 * DMAX
    return [
        lax.dynamic_slice_in_dim(padded, DMAX + sign * (tap - 1) * spacing, length, 1)
        for tap in range(3)
    ]


def conv_apply(padded, weight, spacing, sign, spec):
    taps = shifted_taps(padded, spacing, sign)
    total = dot(spec, taps[0], weight[0])
    for tap in (1, 2):
        total = total + dot(spec, taps[tap], weight[tap])
    return total


def by_partner(value, dim):
    size = lax.axis_size("dp")
    width = value.shape[dim] // size
    place = lax.axis_index("dp")
    return jnp.concatenate(
        [lax.dynamic_slice_in_dim(value, (place ^ m) * width, width, dim) for m in range(size)],
        axis=dim,
    )


def pair_rows(value):
    return jnp.concatenate([value, swap(value, "seq", 1)], axis=0)


def pair_channels(value, ordered):
    half = value.shape[-1] // 2
    core = lax.axis_index("seq") % 2
    if ordered:
        core = core ^ (lax.axis_index("dp") // (lax.axis_size("dp") // 2))
    dim = value.ndim - 1
    mine = lax.dynamic_slice_in_dim(value, core * half, half, dim)
    other = lax.dynamic_slice_in_dim(value, (1 - core) * half, half, dim)
    return jnp.concatenate([mine, swap(other, "seq", 1)], axis=0)


def spread_sum(partial, ordered):
    chips = lax.axis_size("seq") // 2
    rows = partial.shape[1] // chips
    place, layer = lax.axis_index("seq"), lax.axis_index("dp")
    width = 2 * partial.shape[1] // lax.axis_size("dp")
    total = None
    for j in range(chips):
        target = (place // 2) ^ j
        offset = target * rows
        if ordered:
            group = (offset // width) ^ (layer % (lax.axis_size("dp") // 2))
            offset = group * width + offset % width
        block = lax.dynamic_slice_in_dim(partial, offset, rows, 1)
        pairs = [(s, (s % 2) * chips + ((s // 2) ^ j)) for s in range(2 * chips)]
        block = send(block, "seq", pairs).astype(F32)
        total = block if total is None else total + block
    return total


def weight_grad(rows, upstream, spacing, ordered):
    taps = shifted_taps(rows, spacing, 1)
    stacked = jnp.stack([dot("blc,bld->cd", tap, upstream).astype(BF16) for tap in taps])
    return spread_sum(stacked, ordered)


def on_device(embeddings, conv_one, conv_two, head_weight, counts, dilation):
    length = embeddings.shape[1]
    size = lax.axis_size("dp")
    width = conv_one.shape[1]
    batch = counts.shape[0]
    layer = lax.axis_index("dp")
    first_gap, second_gap = dilation[0], dilation[1]
    all_bins = length * lax.axis_size("seq")
    per_layer = embeddings.shape[0]

    def absolute(value):
        stacked = value.reshape((size, per_layer) + value.shape[1:])
        picked = [lax.dynamic_index_in_dim(stacked, layer ^ b, 0, False) for b in range(size)]
        return jnp.concatenate(picked, axis=0)

    groups = [slice(i * batch // GROUPS, (i + 1) * batch // GROUPS) for i in range(GROUPS)]

    blocks = line_gather(embeddings)
    frames = [with_halo(block) for block in blocks]
    pre_one_parts, hidden_parts = [], []
    for block, frame in zip(blocks, frames):
        pre = conv_apply(frame, conv_one, first_gap, 1, "blc,dc->bld")
        own = lax.dynamic_slice_in_dim(block, layer * width, width, 2)
        pre_one_parts.append(pre)
        hidden_parts.append((own.astype(F32) + activate(pre)).astype(BF16))
    framed_in = jnp.concatenate(frames, axis=0)
    hidden_one = absolute(jnp.concatenate(hidden_parts, axis=0))
    pre_one = absolute(jnp.concatenate(pre_one_parts, axis=0))

    conv_two_r = by_partner(conv_two, 2)
    head_r = by_partner(head_weight, 0)
    targets = counts.astype(F32)

    framed_one, pre_two, hidden_two = [], [], []
    for g in groups:
        framed = with_halo(jnp.concatenate(line_gather(hidden_one[g]), axis=2))
        pre = conv_apply(framed, conv_two_r, second_gap, 1, "blc,dc->bld")
        framed_one.append(framed)
        pre_two.append(pre)
        hidden_two.append((hidden_one[g].astype(F32) + activate(pre)).astype(BF16))

    head_rows, logits, stats = [], [], []
    for g, hidden in zip(groups, hidden_two):
        rows = jnp.concatenate(line_gather(hidden), axis=2)
        value = dot("blc,ct->blt", rows, head_r)
        peak = jnp.max(value, axis=1)
        total = jnp.sum(jnp.exp(value - peak[:, None, :]), axis=1)
        cross = jnp.sum(targets[g] * value, axis=1)
        head_rows.append(rows)
        logits.append(value)
        stats.append(jnp.stack([peak, total, jnp.sum(targets[g], axis=1), cross]))

    losses, back_two = [], []
    logit_grads = []
    for g, value, stat in zip(groups, logits, stats):
        every = lax.all_gather(stat, "seq")
        peak = jnp.max(every[:, 0], axis=0)
        total = jnp.sum(every[:, 1] * jnp.exp(every[:, 0] - peak), axis=0)
        count_total = jnp.sum(every[:, 2], axis=0)
        cross_total = jnp.sum(every[:, 3], axis=0)
        log_total = peak + jnp.log(total)
        losses.append((count_total * log_total - cross_total) / all_bins)
        logit_grad = (
            (count_total[:, None] * jnp.exp(value - log_total[:, None]) - targets[g]) / all_bins
        ).astype(BF16)
        logit_grads.append(logit_grad)

    grad_two_out, up_two = [], []
    for i, g in enumerate(groups):
        back = dot("blt,ct->blc", logit_grads[i], head_r).astype(BF16)
        grad = line_scatter(jnp.split(back, size, axis=2))
        grad_two_out.append(grad)
        up_two.append(activate_grad(pre_two[i], grad).astype(BF16))

    head_all = pair_channels(jnp.concatenate(head_rows, axis=0), True)
    grad_all = pair_rows(jnp.concatenate(logit_grads, axis=0))
    head_part = dot("blc,blt->ct", head_all, grad_all).astype(BF16)
    grad_head = spread_sum(head_part[None], True)[0]

    up_one = []
    for i, g in enumerate(groups):
        framed = with_halo(up_two[i])
        back = conv_apply(framed, conv_two_r, second_gap, -1, "bld,dc->blc").astype(BF16)
        grad = grad_two_out[i] + line_scatter(jnp.split(back, size, axis=2))
        up_one.append(activate_grad(pre_one[g], grad).astype(BF16))

    one_all = pair_channels(jnp.concatenate(framed_one, axis=0), True)
    grad_two = weight_grad(one_all, pair_rows(jnp.concatenate(up_two, axis=0)), second_gap, True)

    in_all = pair_channels(framed_in, False)
    up_rel = absolute(jnp.concatenate(up_one, axis=0))
    grad_one = weight_grad(in_all, pair_rows(up_rel), first_gap, False)
    return (jnp.concatenate(losses, axis=0), grad_head, grad_one, grad_two)


def solution(mesh):
    placed = (
        P("dp", "seq", None),
        P(None, "dp", None),
        P(None, "dp", None),
        P(None, "dp"),
        P(None, "seq", "dp"),
        P(),
    )
    return jax.shard_map(
        on_device,
        mesh=mesh,
        in_specs=placed,
        out_specs=(P(None, "dp"), P("seq", "dp"), P(None, "seq", "dp"), P(None, "seq", "dp")),
        check_vma=False,
    )
```

```python
import jax
import jax.numpy as jnp
from jax import lax
from jax.sharding import PartitionSpec as P

DMAX = 32
F32 = jnp.float32
BF16 = jnp.bfloat16


def dot(spec, a, b):
    return jnp.einsum(spec, a, b, preferred_element_type=F32)


def activate(value):
    return jax.nn.gelu(value)


def activate_grad(pre, upstream):
    return jax.vjp(activate, pre)[1](upstream)[0]


def send(value, axis, pairs):
    return lax.ppermute(value, axis, pairs)


def swap(value, axis, mask):
    return send(value, axis, [(i, i ^ mask) for i in range(lax.axis_size(axis))])


def tied(*values):
    return lax.optimization_barrier(values)


def line_gather(block, beside=()):
    size = lax.axis_size("dp")
    if size != 4:
        blocks = [block] + [swap(block, "dp", m) for m in range(1, size)]
        return blocks[:-1], blocks[-1], beside
    far = swap(block, "dp", 2)
    near = swap(block, "dp", 1)
    far, near, beside = tied(far, near, beside)
    return [block, near, far], swap(far, "dp", 1), beside


def line_scatter(chunks, beside=()):
    size = lax.axis_size("dp")
    total = chunks[0].astype(F32)
    if size != 4:
        for m in range(1, size):
            total = total + swap(chunks[m], "dp", m).astype(F32)
        return total, beside
    passed = swap(chunks[3], "dp", 1)
    passed, first, beside = tied(passed, chunks[1], beside)
    far = swap((chunks[2].astype(F32) + passed.astype(F32)).astype(BF16), "dp", 2)
    near = swap(first, "dp", 1)
    return total + near.astype(F32) + far.astype(F32), beside


def exchange_edges(to_last, to_next):
    size = lax.axis_size("seq")
    first = lax.axis_index("seq") % 2 == 0
    inside = swap(jnp.where(first, to_next, to_last), "seq", 1)
    pairs = [(i, i + 1) for i in range(1, size - 1, 2)]
    outside = send(jnp.where(first, to_last, to_next), "seq", pairs + [(j, i) for i, j in pairs])
    return jnp.where(first, outside, inside), jnp.where(first, inside, outside)


def with_halo(value):
    length = value.shape[1]
    before, after = exchange_edges(value[:, :DMAX], value[:, length - DMAX :])
    return jnp.concatenate([before, value, after], axis=1)


def shifted_taps(padded, spacing, sign):
    length = padded.shape[1] - 2 * DMAX
    return [
        lax.dynamic_slice_in_dim(padded, DMAX + sign * (tap - 1) * spacing, length, 1)
        for tap in range(3)
    ]


def taps_sum(padded, weight, spacing, sign, spec):
    taps = shifted_taps(padded, spacing, sign)
    total = dot(spec, taps[0], weight[0])
    for tap in (1, 2):
        total = total + dot(spec, taps[tap], weight[tap])
    return total


def conv_edges(value, weight, spacing):
    length = value.shape[1]
    padded = jnp.pad(value, ((0, 0), (DMAX, DMAX), (0, 0)))
    to_next = lax.dynamic_slice_in_dim(padded, DMAX + length - spacing, DMAX, 1)
    to_last = lax.dynamic_slice_in_dim(padded, spacing, DMAX, 1)
    to_next = dot("blc,dc->bld", to_next, weight[0]).astype(BF16)
    to_last = dot("blc,dc->bld", to_last, weight[2]).astype(BF16)
    before, after = exchange_edges(to_last, to_next)
    total = taps_sum(padded, weight, spacing, 1, "blc,dc->bld")
    edges = jnp.pad(before, ((0, 0), (0, length - DMAX), (0, 0))).astype(F32)
    return total + edges + jnp.pad(after, ((0, 0), (length - DMAX, 0), (0, 0))).astype(F32)


def by_partner(value, dim):
    size = lax.axis_size("dp")
    width = value.shape[dim] // size
    place = lax.axis_index("dp")
    return jnp.concatenate(
        [lax.dynamic_slice_in_dim(value, (place ^ m) * width, width, dim) for m in range(size)],
        axis=dim,
    )


def chip_sum(parts, ordered):
    chips = lax.axis_size("seq") // 2
    core, layer = lax.axis_index("seq") % 2, lax.axis_index("dp")
    rows = parts[0].shape[0] // (2 * chips)
    width = parts[0].shape[0] // lax.axis_size("dp")

    def block(kind, chip):
        offset = (2 * chip + kind) * rows
        if ordered:
            offset = ((offset // width) ^ layer) * width + offset % width
        return jnp.stack([lax.dynamic_slice_in_dim(part, offset, rows, 0) for part in parts])

    given = jnp.stack([block(1 - core, chip) for chip in range(chips)])
    kept = jnp.stack([block(core, chip) for chip in range(chips)])
    return (kept.astype(F32) + swap(given, "seq", 1).astype(F32)).astype(BF16)


def chip_blocks(blocks):
    chip = lax.axis_index("seq") // 2
    return [lax.dynamic_index_in_dim(blocks, chip ^ j, 0, False) for j in range(blocks.shape[0])]


def spread(chosen, steps):
    return [swap(chosen[j], "seq", 2 * j) for j in steps]


def total_of(parts):
    return sum(part.astype(F32) for part in parts)


def channel_blocks(value, ordered):
    chips, chip = lax.axis_size("seq") // 2, lax.axis_index("seq") // 2
    wide = value.shape[2] // chips
    width = value.shape[2] // lax.axis_size("dp")
    received = []
    for j in range(chips):
        offset = (chip ^ j) * wide
        if ordered:
            offset = ((offset // width) ^ lax.axis_index("dp")) * width + offset % width
        block = lax.dynamic_slice_in_dim(value, offset, wide, 2)
        received.append(swap(block, "seq", 2 * j) if j else block)
    return received


def bin_blocks(value):
    chips = lax.axis_size("seq") // 2
    return [value] + [swap(value, "seq", 2 * j) for j in range(1, chips)]


def core_sum(parts):
    stacked = jnp.stack(parts)
    rows = stacked.shape[1] // 2
    core = lax.axis_index("seq") % 2
    kept = lax.dynamic_slice_in_dim(stacked, core * rows, rows, 1)
    given = lax.dynamic_slice_in_dim(stacked, (1 - core) * rows, rows, 1).astype(BF16)
    return kept + swap(given, "seq", 1).astype(F32)


def weight_parts(taps, upstream):
    return [dot("blc,bld->cd", *pair) for pair in zip(taps, upstream)]


def on_device(embeddings, conv_one, conv_two, head_weight, counts, dilation):
    length = embeddings.shape[1]
    size = lax.axis_size("dp")
    width = conv_one.shape[1]
    batch = counts.shape[0]
    layer = lax.axis_index("dp")
    first_gap, second_gap = dilation[0], dilation[1]
    all_bins = length * lax.axis_size("seq")
    per_layer = embeddings.shape[0]

    def absolute(value):
        stacked = value.reshape((size, per_layer) + value.shape[1:])
        picked = [lax.dynamic_index_in_dim(stacked, layer ^ b, 0, False) for b in range(size)]
        return jnp.concatenate(picked, axis=0)

    def layer_one(blocks):
        value = jnp.concatenate(blocks, axis=0)
        frame = with_halo(value)
        pre = taps_sum(frame, conv_one, first_gap, 1, "blc,dc->bld")
        own = lax.dynamic_slice_in_dim(value, layer * width, width, 2)
        return frame, pre, (own.astype(F32) + activate(pre)).astype(BF16)

    early, late, _ = line_gather(embeddings)
    made = [layer_one(early), layer_one([late])]
    framed_in, pre_one, hidden_one = [jnp.concatenate(some, axis=0) for some in zip(*made)]
    pre_one, hidden_one = absolute(pre_one), absolute(hidden_one)

    conv_two_r = by_partner(conv_two, 2)
    head_r = by_partner(head_weight, 0)
    targets = counts.astype(F32)

    hidden_one, framed_in = tied(hidden_one, framed_in)
    in_blocks = channel_blocks(framed_in, False)
    early, late, _ = line_gather(hidden_one)
    rows_one = jnp.concatenate(early + [late], axis=2)
    rows_one, in_blocks[:-1] = tied(rows_one, in_blocks[:-1])
    pre_two = conv_edges(rows_one, conv_two_r, second_gap)
    hidden_two = (hidden_one.astype(F32) + activate(pre_two)).astype(BF16)

    hidden_two, rows_one, in_blocks[-1] = tied(hidden_two, rows_one, in_blocks[-1])
    one_blocks = channel_blocks(rows_one, True)
    early, late, _ = line_gather(hidden_two)
    rows_two = jnp.concatenate(early + [late], axis=2)
    rows_two, one_blocks[:-1] = tied(rows_two, one_blocks[:-1])
    logits = dot("blc,ct->blt", rows_two, head_r)
    peak = jnp.max(logits, axis=1)
    total = jnp.sum(jnp.exp(logits - peak[:, None, :]), axis=1)
    cross = jnp.sum(targets * logits, axis=1)
    every = lax.all_gather(jnp.stack([peak, total, jnp.sum(targets, axis=1), cross]), "seq")
    every, one_blocks[-1] = tied(every, one_blocks[-1])
    one_blocks, in_blocks = jnp.concatenate(one_blocks, axis=0), jnp.concatenate(in_blocks, axis=0)
    peak = jnp.max(every[:, 0], axis=0)
    total = jnp.sum(every[:, 1] * jnp.exp(every[:, 0] - peak), axis=0)
    count_total = jnp.sum(every[:, 2], axis=0)
    cross_total = jnp.sum(every[:, 3], axis=0)
    log_total = peak + jnp.log(total)
    track_loss = (count_total * log_total - cross_total) / all_bins
    logit_grad = (
        (count_total[:, None] * jnp.exp(logits - log_total[:, None]) - targets) / all_bins
    ).astype(BF16)

    back = dot("blt,ct->blc", logit_grad, head_r).astype(BF16)
    logit_grad, back = tied(logit_grad, back)
    head_part = dot("blc,blt->ct", rows_two, logit_grad).astype(BF16)
    head_blocks = chip_blocks(chip_sum([head_part], True))
    near_steps, far_steps = range(1, len(head_blocks) - 1), range(len(head_blocks) - 1, len(head_blocks))
    head_near, head_far = spread(head_blocks, near_steps), spread(head_blocks, far_steps)
    grad_two_out, _ = line_scatter(jnp.split(back, size, axis=2))
    up_two = activate_grad(pre_two, grad_two_out).astype(BF16)
    up_two, head_near = tied(up_two, head_near)

    framed_back = with_halo(up_two)
    back = taps_sum(framed_back, conv_two_r, second_gap, -1, "bld,dc->blc").astype(BF16)
    framed_back, back, head_far = tied(framed_back, back, head_far)
    grad_head = total_of(head_blocks[:1] + head_near + head_far)[0]
    back_blocks = bin_blocks(framed_back)
    summed, back_blocks[:-1] = line_scatter(jnp.split(back, size, axis=2), back_blocks[:-1])
    summed, back_blocks[-1] = tied(summed, back_blocks[-1])
    up_taps = shifted_taps(jnp.concatenate(back_blocks, axis=0), second_gap, -1)
    grad_two = core_sum(weight_parts([one_blocks] * 3, up_taps))

    up_one = absolute(activate_grad(pre_one, grad_two_out + summed).astype(BF16))
    up_blocks = bin_blocks(up_one)
    up_all = jnp.concatenate(up_blocks, axis=0)
    grad_one = core_sum(weight_parts(shifted_taps(in_blocks, first_gap, 1), [up_all] * 3))
    return (track_loss, grad_head, grad_one, grad_two)


def solution(mesh):
    placed = (
        P("dp", "seq", None),
        P(None, "dp", None),
        P(None, "dp", None),
        P(None, "dp"),
        P(None, "seq", "dp"),
        P(),
    )
    return jax.shard_map(
        on_device,
        mesh=mesh,
        in_specs=placed,
        out_specs=(P(None, "dp"), P("seq", "dp"), P(None, "seq", "dp"), P(None, "seq", "dp")),
        check_vma=False,
    )
```

```python
import jax
import jax.numpy as jnp
from jax import lax
from jax.sharding import PartitionSpec as P

DMAX = 32
F32 = jnp.float32
BF16 = jnp.bfloat16


def dot(spec, a, b):
    return jnp.einsum(spec, a, b, preferred_element_type=F32)


def activate(value):
    return jax.nn.gelu(value)


def activate_grad(pre, upstream):
    return jax.vjp(activate, pre)[1](upstream)[0]


def send(value, axis, pairs):
    return lax.ppermute(value, axis, pairs)


def swap(value, axis, mask):
    return send(value, axis, [(i, i ^ mask) for i in range(lax.axis_size(axis))])


def tied(*values):
    return lax.optimization_barrier(values)


def line_gather(block, beside=()):
    size = lax.axis_size("dp")
    if size != 4:
        blocks = [block] + [swap(block, "dp", m) for m in range(1, size)]
        return blocks[:-1], blocks[-1], beside
    far = swap(block, "dp", 2)
    near = swap(block, "dp", 1)
    far, near, beside = tied(far, near, beside)
    return [block, near, far], swap(far, "dp", 1), beside


def line_scatter(chunks, beside=()):
    size = lax.axis_size("dp")
    total = chunks[0].astype(F32)
    if size != 4:
        for m in range(1, size):
            total = total + swap(chunks[m], "dp", m).astype(F32)
        return total, beside
    passed = swap(chunks[3], "dp", 1)
    passed, first, beside = tied(passed, chunks[1], beside)
    far = swap((chunks[2].astype(F32) + passed.astype(F32)).astype(BF16), "dp", 2)
    near = swap(first, "dp", 1)
    return total + near.astype(F32) + far.astype(F32), beside


def exchange_edges(to_last, to_next):
    size = lax.axis_size("seq")
    first = lax.axis_index("seq") % 2 == 0
    inside = swap(jnp.where(first, to_next, to_last), "seq", 1)
    pairs = [(i, i + 1) for i in range(1, size - 1, 2)]
    outside = send(jnp.where(first, to_last, to_next), "seq", pairs + [(j, i) for i, j in pairs])
    return jnp.where(first, outside, inside), jnp.where(first, inside, outside)


def with_halo(value):
    length = value.shape[1]
    before, after = exchange_edges(value[:, :DMAX], value[:, length - DMAX :])
    return jnp.concatenate([before, value, after], axis=1)


def shifted_taps(padded, spacing, sign):
    length = padded.shape[1] - 2 * DMAX
    return [
        lax.dynamic_slice_in_dim(padded, DMAX + sign * (tap - 1) * spacing, length, 1)
        for tap in range(3)
    ]


def taps_sum(padded, weight, spacing, sign, spec):
    taps = shifted_taps(padded, spacing, sign)
    total = dot(spec, taps[0], weight[0])
    for tap in (1, 2):
        total = total + dot(spec, taps[tap], weight[tap])
    return total


def conv_edges(value, weight, spacing):
    length = value.shape[1]
    padded = jnp.pad(value, ((0, 0), (DMAX, DMAX), (0, 0)))
    to_next = lax.dynamic_slice_in_dim(padded, DMAX + length - spacing, DMAX, 1)
    to_last = lax.dynamic_slice_in_dim(padded, spacing, DMAX, 1)
    to_next = dot("blc,dc->bld", to_next, weight[0]).astype(BF16)
    to_last = dot("blc,dc->bld", to_last, weight[2]).astype(BF16)
    before, after = exchange_edges(to_last, to_next)
    total = taps_sum(padded, weight, spacing, 1, "blc,dc->bld")
    edges = jnp.pad(before, ((0, 0), (0, length - DMAX), (0, 0))).astype(F32)
    return total + edges + jnp.pad(after, ((0, 0), (length - DMAX, 0), (0, 0))).astype(F32)


def by_partner(value, dim):
    size = lax.axis_size("dp")
    width = value.shape[dim] // size
    place = lax.axis_index("dp")
    return jnp.concatenate(
        [lax.dynamic_slice_in_dim(value, (place ^ m) * width, width, dim) for m in range(size)],
        axis=dim,
    )


def chip_sums(part, ordered):
    chips, chip = lax.axis_size("seq") // 2, lax.axis_index("seq") // 2
    core, layer = lax.axis_index("seq") % 2, lax.axis_index("dp")
    rows = part.shape[0] // (2 * chips)
    width = part.shape[0] // lax.axis_size("dp")

    def block(kind, target):
        offset = (2 * target + kind) * rows
        if ordered:
            offset = ((offset // width) ^ layer) * width + offset % width
        return lax.dynamic_slice_in_dim(part, offset, rows, 0)

    return [
        (block(core, chip ^ j).astype(F32) + swap(block(1 - core, chip ^ j), "seq", 1).astype(F32)).astype(BF16)
        for j in range(chips)
    ]


def spread(chosen, steps):
    return [swap(chosen[j], "seq", 2 * j) for j in steps]


def total_of(parts):
    return sum(part.astype(F32) for part in parts)


def channel_blocks(value, ordered):
    chips, chip = lax.axis_size("seq") // 2, lax.axis_index("seq") // 2
    wide = value.shape[2] // chips
    width = value.shape[2] // lax.axis_size("dp")
    received = []
    for j in range(chips):
        offset = (chip ^ j) * wide
        if ordered:
            offset = ((offset // width) ^ lax.axis_index("dp")) * width + offset % width
        block = lax.dynamic_slice_in_dim(value, offset, wide, 2)
        received.append(swap(block, "seq", 2 * j) if j else block)
    return received


def bin_blocks(value):
    chips = lax.axis_size("seq") // 2
    return [value] + [swap(value, "seq", 2 * j) for j in range(1, chips)]


def core_sum(parts):
    stacked = jnp.stack(parts)
    rows = stacked.shape[1] // 2
    core = lax.axis_index("seq") % 2
    kept = lax.dynamic_slice_in_dim(stacked, core * rows, rows, 1)
    given = lax.dynamic_slice_in_dim(stacked, (1 - core) * rows, rows, 1).astype(BF16)
    return kept + swap(given, "seq", 1).astype(F32)


def weight_parts(taps, upstream):
    return [dot("blc,bld->cd", *pair) for pair in zip(taps, upstream)]


def on_device(embeddings, conv_one, conv_two, head_weight, counts, dilation):
    length = embeddings.shape[1]
    size = lax.axis_size("dp")
    width = conv_one.shape[1]
    batch = counts.shape[0]
    layer = lax.axis_index("dp")
    first_gap, second_gap = dilation[0], dilation[1]
    all_bins = length * lax.axis_size("seq")
    per_layer = embeddings.shape[0]

    def absolute(value):
        stacked = value.reshape((size, per_layer) + value.shape[1:])
        picked = [lax.dynamic_index_in_dim(stacked, layer ^ b, 0, False) for b in range(size)]
        return jnp.concatenate(picked, axis=0)

    def layer_one(blocks):
        value = jnp.concatenate(blocks, axis=0)
        frame = with_halo(value)
        pre = taps_sum(frame, conv_one, first_gap, 1, "blc,dc->bld")
        own = lax.dynamic_slice_in_dim(value, layer * width, width, 2)
        return frame, pre, (own.astype(F32) + activate(pre)).astype(BF16)

    early, late, _ = line_gather(embeddings)
    made = [layer_one(early), layer_one([late])]
    framed_in, pre_one, hidden_one = [jnp.concatenate(some, axis=0) for some in zip(*made)]
    pre_one, hidden_one = absolute(pre_one), absolute(hidden_one)

    conv_two_r = by_partner(conv_two, 2)
    head_r = by_partner(head_weight, 0)
    targets = counts.astype(F32)

    hidden_one, framed_in = tied(hidden_one, framed_in)
    in_blocks = channel_blocks(framed_in, False)
    early, late, _ = line_gather(hidden_one)
    early = jnp.concatenate(early, axis=2)
    known = early.shape[2]
    late, in_blocks[:-1] = tied(late, in_blocks[:-1])
    pre_two = conv_edges(early, conv_two_r[:, :, :known], second_gap)
    pre_two = pre_two + taps_sum(with_halo(late), conv_two_r[:, :, known:], second_gap, 1, "blc,dc->bld")
    rows_one = jnp.concatenate([early, late], axis=2)
    hidden_two = (hidden_one.astype(F32) + activate(pre_two)).astype(BF16)

    hidden_two, rows_one, in_blocks[-1] = tied(hidden_two, rows_one, in_blocks[-1])
    one_blocks = channel_blocks(rows_one, True)
    early, late, one_blocks[:-1] = line_gather(hidden_two, one_blocks[:-1])
    early = jnp.concatenate(early, axis=2)
    rows_two = jnp.concatenate([early, late], axis=2)
    logits = dot("blc,ct->blt", early, head_r[:known]) + dot("blc,ct->blt", late, head_r[known:])
    peak = jnp.max(logits, axis=1)
    total = jnp.sum(jnp.exp(logits - peak[:, None, :]), axis=1)
    cross = jnp.sum(targets * logits, axis=1)
    every = lax.all_gather(jnp.stack([peak, total, jnp.sum(targets, axis=1), cross]), "seq")
    every, one_blocks[-1] = tied(every, one_blocks[-1])
    one_blocks, in_blocks = jnp.concatenate(one_blocks, axis=0), jnp.concatenate(in_blocks, axis=0)
    peak = jnp.max(every[:, 0], axis=0)
    total = jnp.sum(every[:, 1] * jnp.exp(every[:, 0] - peak), axis=0)
    count_total = jnp.sum(every[:, 2], axis=0)
    cross_total = jnp.sum(every[:, 3], axis=0)
    log_total = peak + jnp.log(total)
    track_loss = (count_total * log_total - cross_total) / all_bins
    logit_grad = (
        (count_total[:, None] * jnp.exp(logits - log_total[:, None]) - targets) / all_bins
    ).astype(BF16)

    back = dot("blt,ct->blc", logit_grad, head_r).astype(BF16)
    logit_grad, back = tied(logit_grad, back)
    head_part = dot("blc,blt->ct", rows_two, logit_grad).astype(BF16)
    head_blocks = chip_sums(head_part, True)
    near_steps, far_steps = range(1, len(head_blocks) - 1), range(len(head_blocks) - 1, len(head_blocks))
    head_near, head_far = spread(head_blocks, near_steps), spread(head_blocks, far_steps)
    grad_two_out, _ = line_scatter(jnp.split(back, size, axis=2))
    up_two = activate_grad(pre_two, grad_two_out).astype(BF16)
    up_two, head_near = tied(up_two, head_near)

    framed_back = with_halo(up_two)
    back = taps_sum(framed_back, conv_two_r, second_gap, -1, "bld,dc->blc").astype(BF16)
    framed_back, back, head_far = tied(framed_back, back, head_far)
    grad_head = total_of(head_blocks[:1] + head_near + head_far)
    back_blocks = bin_blocks(framed_back)
    summed, back_blocks[:-1] = line_scatter(jnp.split(back, size, axis=2), back_blocks[:-1])
    summed, back_blocks[-1] = tied(summed, back_blocks[-1])
    up_taps = shifted_taps(jnp.concatenate(back_blocks, axis=0), second_gap, -1)
    grad_two = core_sum(weight_parts([one_blocks] * 3, up_taps))

    up_one = absolute(activate_grad(pre_one, grad_two_out + summed).astype(BF16))
    up_blocks = bin_blocks(up_one)
    up_all = jnp.concatenate(up_blocks, axis=0)
    grad_one = core_sum(weight_parts(shifted_taps(in_blocks, first_gap, 1), [up_all] * 3))
    return (track_loss, grad_head, grad_one, grad_two)


def solution(mesh):
    placed = (
        P("dp", "seq", None),
        P(None, "dp", None),
        P(None, "dp", None),
        P(None, "dp"),
        P(None, "seq", "dp"),
        P(),
    )
    return jax.shard_map(
        on_device,
        mesh=mesh,
        in_specs=placed,
        out_specs=(P(None, "dp"), P("seq", "dp"), P(None, "seq", "dp"), P(None, "seq", "dp")),
        check_vma=False,
    )
```
